32 devices in a mesh: tm: 4 (over x, core), inp: 8 (over z, y).
Axes of the slice: x: 2, y: 2, z: 4, core: 2. Of those that a mesh axis runs over, the one named last changes fastest.
Arguments:
- voltage: int32 [256, 524288], P('inp', 'tm'), may hold values from -127 to 127
- taps: float32 [4, 512], replicated, may hold values from -0.0625 to 0.0625
- chan_table: int32 [256], replicated, may hold values from 0 to 255, each once
Outputs:
- visibility: float32 [256, 128, 256], P('tm', 'inp')
- beam: float32 [128, 1024], P('inp', 'tm')
The draws below stay inside these ranges and needn't reach their ends.
Inputs may be any that keep to these rules, and one draw needn't show every extreme that they name: `chan_table`: each channel number appears once.
All inputs are finite; a program needn't handle non-finite values.
Results may differ from the reference program's by a relative error of at most 0.0016.
Values may be sent and summed in bfloat16 or wider, within the bound.
No kernel may reach another device: no remote copies, remote signals or barrier semaphores. Data moves between devices by JAX's collectives and lax.ppermute only.
A program may use at most 64 MiB of HBM per device.

```python
import math
import jax
import jax.numpy as jnp
from jax import lax

NIN = 256
P_SIZE = 512
TAPS = 4
NCH = 128
BAND = 256
SAMPLES = 524288


def draw_voltage(key, part):
    first, second = jax.random.split(jax.random.fold_in(key, 11))
    amplitude = jnp.minimum(jax.random.randint(first, (NIN, 1), 12, 160), 127).astype(jnp.int32)
    return jax.random.randint(second, (NIN, SAMPLES), -amplitude, amplitude + 1).astype(jnp.int32)


def normal_values(rng, extent, spread, bound, held_as=jnp.bfloat16):
    result = spread * jax.random.normal(rng, extent, jnp.float32)
    return jnp.clip(result, min=-bound, max=bound).astype(held_as)


def setup_inputs(seed: int = 0) -> dict:
    key_list = jax.random.split(jax.random.key(seed), 4)
    return {
        "voltage": draw_voltage(jax.random.fold_in(key_list[3], 71), 0),
        "taps": normal_values(key_list[1], (TAPS, P_SIZE), 0.01, 0.0625, jnp.float32),
        "chan_table": jax.random.permutation(key_list[2], BAND).astype(jnp.int32),
    }


def dft_table(chan_table):
    chosen = chan_table[:NCH].astype(jnp.int32)
    points = jnp.arange(P_SIZE, dtype=jnp.int32)
    phase = chosen[:, None] * points[None, :] % P_SIZE
    angle = phase.astype(jnp.float32) * (2.0 * math.pi / P_SIZE)
    factor = 1.0 / math.sqrt(P_SIZE)
    table = jnp.stack([jnp.cos(angle) * factor, -jnp.sin(angle) * factor], axis=1)
    return table.astype(jnp.bfloat16)

def reference(voltage, taps, chan_table):
    table = dft_table(chan_table)
    total = voltage.shape[1] // P_SIZE
    group_rows = 16

    def channelize(block):
        volts = block.astype(jnp.float32).reshape(group_rows, total, P_SIZE)
        padded = jnp.concatenate([jnp.zeros((group_rows, TAPS - 1, P_SIZE), jnp.float32), volts], axis=1)
        filtered = jnp.zeros((group_rows, total, P_SIZE), jnp.float32)
        for tap_index in range(TAPS):
            filtered = filtered + taps[tap_index] * padded[:, tap_index:tap_index + total, :]
        filtered = filtered.astype(jnp.bfloat16)
        spectra = jnp.einsum('cqp,isp->cqis', table.astype(jnp.float32), filtered.astype(jnp.float32), preferred_element_type=jnp.float32)
        return spectra.astype(jnp.bfloat16)
    blocks = voltage.reshape(NIN // group_rows, group_rows, voltage.shape[1])
    spectra = lax.map(channelize, blocks)
    spectra = jnp.transpose(spectra, (1, 2, 0, 3, 4)).reshape(NCH, 2, NIN, total)
    upper = jnp.arange(NIN, dtype=jnp.int32)[:, None] <= jnp.arange(NIN, dtype=jnp.int32)[None, :]

    def correlate(parts):
        real_in = parts[0].astype(jnp.float32)
        imag_in = parts[1].astype(jnp.float32)
        combined = jnp.concatenate([real_in, imag_in], axis=1)
        rotated = jnp.concatenate([imag_in, -real_in], axis=1)
        re_part = jnp.dot(combined, combined.T, preferred_element_type=jnp.float32)
        im_part = jnp.dot(rotated, combined.T, preferred_element_type=jnp.float32)
        packed = jnp.where(upper, re_part, im_part) / total
        power = lax.optimization_barrier(jnp.sum(parts.astype(jnp.float32) ** 2, axis=(0, 1))) / NIN
        return (packed, power)
    packed_all, beam = lax.map(correlate, spectra)
    visibility = jnp.transpose(packed_all, (1, 0, 2))
    return (visibility, beam)
```

```python
import functools
import math

import jax
import jax.numpy as jnp
from jax import lax
from jax.experimental import pallas as pl
from jax.experimental.pallas import tpu as pltpu
from jax.sharding import PartitionSpec as P

P_SIZE = 512
TAPS = 4
NCH = 128
LANES = 128
ROWS = 8
PIECES = P_SIZE // LANES
VMEM_BYTES = 50 * 1024 * 1024
SMALL_BYTES = 20 * 1024 * 1024


def odd_rows(rows):
    tiles = rows // ROWS
    return (tiles + 1 - tiles % 2) * ROWS


def write_table(chan_ref, table):
    chosen = chan_ref[pl.ds(0, 1), :].astype(jnp.float32)
    chosen = jnp.broadcast_to(chosen, (NCH, LANES)).T.astype(jnp.int32)
    factor = 1.0 / math.sqrt(P_SIZE)
    quarter = P_SIZE // 4
    for n in range(PIECES):
        points = lax.broadcasted_iota(jnp.int32, (NCH, LANES), 1) + n * LANES
        phase = (chosen * points) & (P_SIZE - 1)
        turned = phase + quarter // 2
        quadrant = (turned // quarter) & 3
        x = ((turned & (quarter - 1)) - quarter // 2).astype(jnp.float32)
        x = x * (2.0 * math.pi / P_SIZE)
        z = x * x
        sine = x + x * z * (
            -1.6666654611e-1 + z * (8.3321608736e-3 + z * -1.9515295891e-4)
        )
        cosine = 1.0 - 0.5 * z + z * z * (
            4.166664568298827e-2 + z * (-1.388731625493765e-3 + z * 2.443315711809948e-5)
        )
        odd = (quadrant & 1) == 1
        real = jnp.where(odd, sine, cosine)
        imag = jnp.where(odd, cosine, sine)
        real = jnp.where((quadrant == 1) | (quadrant == 2), -real, real)
        imag = jnp.where(quadrant >= 2, imag, -imag)
        at = pl.ds(n * LANES, LANES)
        table[pl.ds(0, NCH), at] = (real * factor).astype(jnp.bfloat16)
        table[pl.ds(NCH, NCH), at] = (imag * factor).astype(jnp.bfloat16)


def channelize_kernel(opening, groups, plan, volts_ref, *refs):
    if opening:
        chan_hbm, taps_hbm, *refs = refs
        *outs, table_ref, tail_ref, taps_ref, chan_ref, held, filt, spec, sems = refs
    else:
        halo_ref, taps_ref, table_ref, *refs = refs
        *outs, held, filt, spec, sems = refs
    blocks, extent = held.shape[0], held.shape[1]
    span = extent - (TAPS - 1)
    inputs = blocks * ROWS
    slots = NCH // groups
    pitch, depth = odd_rows(span), odd_rows(inputs)
    me = lax.axis_index("inp")

    def copy_of(b):
        if opening:
            source = volts_ref.at[b, pl.ds(volts_ref.shape[1] - extent, extent)]
            target = held.at[b]
        else:
            source = volts_ref.at[b, pl.ds(0, span)]
            target = held.at[b, pl.ds(TAPS - 1, span)]
        return pltpu.make_async_copy(source, target, sems.at[b])

    if opening:
        chan_copy = pltpu.make_async_copy(chan_hbm, chan_ref, sems.at[blocks])
        taps_copy = pltpu.make_async_copy(taps_hbm, taps_ref, sems.at[blocks + 1])
        chan_copy.start()
        taps_copy.start()
    for b in range(blocks):
        copy_of(b).start()
    if opening:
        chan_copy.wait()
        write_table(chan_ref, table_ref)
        taps_copy.wait()

    def one_block(b, carry):
        copy_of(b).wait()
        taps = [
            [
                jnp.broadcast_to(taps_ref[pl.ds(k, 1), pl.ds(n * LANES, LANES)], (ROWS, LANES))
                for n in range(PIECES)
            ]
            for k in range(TAPS)
        ]
        if opening:
            for k in range(TAPS - 1):
                for n in range(PIECES):
                    tail_ref[b, k, n] = held[b, span + k, n].astype(jnp.float32)
            before = [
                [held[b, k, n].astype(jnp.float32) for n in range(PIECES)]
                for k in range(TAPS - 1)
            ]
        else:
            before = [[halo_ref[b, k, n] for n in range(PIECES)] for k in range(TAPS - 1)]

        def filter_step(step, window):
            window = [list(w) for w in window]
            for u in range(ROWS):
                s = step * ROWS + u
                now = [held[b, s + TAPS - 1, n].astype(jnp.float32) for n in range(PIECES)]
                window = window + [now]
                for n in range(PIECES):
                    total = taps[0][n] * window[0][n]
                    for k in range(1, TAPS):
                        total = total + taps[k][n] * window[k][n]
                    filt[n, pl.ds(s, ROWS, stride=pitch), :] = total
                window = window[1:]
            return window

        lax.fori_loop(0, span // ROWS, filter_step, before)

        def transform(pair, carry):
            rows = []
            for e in range(2):
                at = pl.ds(pl.multiple_of((pair * 2 + e) * pitch, ROWS), span)
                line = [filt[n, at, :].astype(jnp.bfloat16) for n in range(PIECES)]
                rows.append(jnp.concatenate(line, axis=1))
            out = lax.dot_general(
                table_ref[...],
                jnp.concatenate(rows, axis=0),
                (((1,), (1,)), ((), ())),
                preferred_element_type=jnp.float32,
            )
            for e in range(2):
                i = b * ROWS + pair * 2 + e
                spec[pl.ds(i, 2 * NCH, stride=depth), :] = out[:, e * span : (e + 1) * span]
            return carry

        return lax.fori_loop(0, ROWS // 2, transform, carry)

    lax.fori_loop(0, blocks, one_block, 0)
    for out, pieces in zip(outs, plan):
        count = out.shape[1]
        for place, (j, first) in enumerate(pieces):
            for q in range(2):
                there = j if opening else me ^ j
                start = (q * NCH + there * slots + first) * depth
                rows = spec[pl.ds(pl.multiple_of(start, depth), count * depth), :]
                rows = rows.reshape(count, depth, span)[:, :inputs]
                out[place, :, pl.ds(q * inputs, inputs), :] = rows.astype(jnp.bfloat16)


def channelize(volts, extra, groups, plan, counts):
    opening = len(extra) == 2
    blocks, spectra = volts.shape[:2]
    span = spectra // 2
    inputs = blocks * ROWS
    whole = pl.BlockSpec(memory_space=pltpu.VMEM)
    far = pl.BlockSpec(memory_space=pltpu.HBM)
    out_shape = [
        jax.ShapeDtypeStruct((len(pieces), count, 2 * inputs, span), jnp.bfloat16)
        for pieces, count in zip(plan, counts)
    ]
    scratch = [
        pltpu.VMEM((blocks, span + TAPS - 1, PIECES, ROWS, LANES), jnp.int32),
        pltpu.VMEM((PIECES, ROWS * odd_rows(span), LANES), jnp.float32),
        pltpu.VMEM((2 * NCH * odd_rows(inputs), span), jnp.float32),
        pltpu.SemaphoreType.DMA((blocks + 2,)),
    ]
    if opening:
        out_shape.append(jax.ShapeDtypeStruct((2 * NCH, P_SIZE), jnp.bfloat16))
        out_shape.append(
            jax.ShapeDtypeStruct((blocks, TAPS - 1, PIECES, ROWS, LANES), jnp.float32)
        )
        out_shape.append(jax.ShapeDtypeStruct((TAPS, P_SIZE), jnp.float32))
        scratch = [pltpu.VMEM(extra[0].shape, jnp.int32)] + scratch
    in_specs = [far, far, far] if opening else [far, whole, whole, whole]
    moved = blocks * ROWS * span * P_SIZE * 4 + 2 * NCH * inputs * span * 2
    return pl.pallas_call(
        functools.partial(channelize_kernel, opening, groups, plan),
        out_shape=out_shape,
        in_specs=in_specs,
        out_specs=[whole] * len(out_shape),
        scratch_shapes=scratch,
        compiler_params=pltpu.CompilerParams(vmem_limit_bytes=VMEM_BYTES),
        cost_estimate=pl.CostEstimate(flops=1000, bytes_accessed=12000000, transcendentals=0),
    )(volts, *extra)


def correlate_kernel(groups, others, first, total, places, *refs):
    *parts, beam, stack = refs[-others - 2 :]
    channels = beam.shape[0]
    everyone = parts[0].shape[-1]
    inputs = everyone // groups
    span = beam.shape[1] // 2
    rows_each = everyone // others
    me = lax.axis_index("inp")
    here = lax.axis_index("tm")

    def one_channel(c, carry):
        for j in range(groups):
            at = pl.ds(pl.multiple_of((me ^ j) * inputs, inputs), inputs)
            for h in range(2):
                operand, index, start = (places[j], 0, 0) if h == 0 else (0, me ^ j, first)
                for q in range(2):
                    piece = refs[operand][index, start + c, pl.ds(q * inputs, inputs), :]
                    stack[at, pl.ds((2 * h + q) * span, span)] = piece.astype(stack.dtype)
        values = stack[...].astype(jnp.bfloat16)
        wide = values.astype(jnp.float32)
        power = jnp.sum(wide * wide, axis=0, keepdims=True)
        power = jnp.concatenate(
            [
                power[:, 2 * h * span : (2 * h + 1) * span]
                + power[:, (2 * h + 1) * span : (2 * h + 2) * span]
                for h in range(2)
            ],
            axis=1,
        )
        beam[pl.ds(c, 1), :] = power * (1.0 / everyone)
        col = lax.broadcasted_iota(jnp.int32, (rows_each, everyone), 1)
        row = lax.broadcasted_iota(jnp.int32, (rows_each, everyone), 0)
        for k in range(others):
            base = (here ^ k) * rows_each
            some = stack[pl.ds(pl.multiple_of(base, rows_each), rows_each), :]
            some = some.astype(jnp.bfloat16)
            turned = jnp.concatenate(
                [
                    part
                    for h in range(2)
                    for part in (
                        some[:, (2 * h + 1) * span : (2 * h + 2) * span],
                        -some[:, 2 * h * span : (2 * h + 1) * span],
                    )
                ],
                axis=1,
            )
            both = lax.dot_general(
                jnp.concatenate([some, turned], axis=0),
                values,
                (((1,), (1,)), ((), ())),
                preferred_element_type=jnp.float32,
            )
            packed = jnp.where(row + base <= col, both[:rows_each], both[rows_each:])
            parts[k][c] = (packed * (1.0 / total)).astype(parts[k].dtype)
        return carry

    lax.fori_loop(0, channels, one_channel, 0)


def exchange_order(others):
    order = [0]
    distance = others // 2
    while distance >= 1:
        order = order + [k + distance for k in order]
        distance //= 2
    return order


def correlate(operands, places, groups, first, channels, others, total):
    double, span = operands[0].shape[-2:]
    everyone = double // 2 * groups
    rows_each = everyone // others
    whole = pl.BlockSpec(memory_space=pltpu.VMEM)
    shape = (channels, rows_each, everyone)
    parts = [jax.ShapeDtypeStruct(shape, jnp.float32)]
    parts += [jax.ShapeDtypeStruct(shape, jnp.bfloat16)] * (others - 1)
    held = jnp.bfloat16 if double % 32 == 0 else jnp.float32
    return pl.pallas_call(
        functools.partial(correlate_kernel, groups, others, first, total, places),
        out_shape=parts + [jax.ShapeDtypeStruct((channels, 2 * span), jnp.float32)],
        in_specs=[whole] * len(operands),
        out_specs=[whole] * (others + 1),
        scratch_shapes=[pltpu.VMEM((everyone, 4 * span), held)],
        compiler_params=pltpu.CompilerParams(vmem_limit_bytes=SMALL_BYTES),
        cost_estimate=pl.CostEstimate(flops=1000, bytes_accessed=100000000, transcendentals=0),
    )(*operands)


def finish_kernel(cuts, *refs):
    out = refs[-1]
    for at, (first, count) in enumerate(cuts):
        step = (len(refs) - 1) // len(cuts) - 1
        came = refs[len(cuts) + at * step : len(cuts) + (at + 1) * step]
        for c in range(count):
            total = refs[at][c]
            for part in came:
                total = total + part[c].astype(jnp.float32)
            out[:, first + c, :] = total


def finish(kept, came, cuts):
    rows_each, everyone = kept[0].shape[1:]
    slots = sum(count for _, count in cuts)
    whole = pl.BlockSpec(memory_space=pltpu.VMEM)
    return pl.pallas_call(
        functools.partial(finish_kernel, cuts),
        out_shape=jax.ShapeDtypeStruct((rows_each, slots, everyone), jnp.float32),
        in_specs=[whole] * (len(kept) + len(came)),
        out_specs=whole,
        cost_estimate=pl.CostEstimate(flops=1000, bytes_accessed=1000, transcendentals=0),
        compiler_params=pltpu.CompilerParams(vmem_limit_bytes=SMALL_BYTES),
    )(*kept, *came)


def swapped(block, axis, distance):
    devices = range(lax.axis_size(axis))
    return lax.ppermute(block, axis, [(i, i ^ distance) for i in devices])


def after(block, *earlier):
    if not earlier:
        return block
    return lax.optimization_barrier((block, *earlier))[0]


def send_order(groups):
    half = groups // 2
    return list(range(half, groups)) + list(range(1, half))


def channel_cuts(slots):
    sizes = [8, 8] if slots == 16 else [slots]
    firsts = [sum(sizes[:n]) for n in range(len(sizes))]
    return list(zip(firsts, sizes))


def on_device(voltage, taps, chan_table):
    inputs = voltage.shape[0]
    spectra = voltage.shape[1] // P_SIZE
    groups = lax.axis_size("inp")
    others = lax.axis_size("tm")
    slots = NCH // groups
    total = spectra * others
    cuts = channel_cuts(slots)
    volts = voltage.reshape(inputs // ROWS, ROWS, spectra, PIECES, LANES)
    volts = jnp.transpose(volts, (0, 2, 3, 1, 4))

    plan = [[(d, 0) for d in range(groups)]]
    late, table, tail, taps = channelize(
        volts, (chan_table.reshape(-1, LANES), taps), groups, plan, [slots]
    )
    late = lax.all_to_all(late, "inp", split_axis=0, concat_axis=0, tiled=True)
    devices = range(others)
    halo = lax.ppermute(tail, "tm", [(i - 1, i) for i in devices if i > 0])

    plan, counts = [], []
    for first, count in cuts:
        plan += [[(j, first)] for j in range(groups)]
        counts += [count] * groups
    early = channelize(volts, (halo, taps, table), groups, plan, counts)

    order = send_order(groups)
    kept, came, beams = [], [], []
    for at, (first, count) in enumerate(cuts):
        mine = early[at * groups : (at + 1) * groups]
        got = [swapped(mine[j], "inp", j) for j in order]
        operands = [late, mine[0]] + got
        places = [1] + [2 + order.index(j) for j in range(1, groups)]
        *parts, beam = correlate(operands, places, groups, first, count, others, total)
        kept.append(parts[0])
        came.append([swapped(parts[k], "tm", k) for k in range(1, others)])
        beams.append(beam)
    visibility = finish(kept, sum(came, []), cuts)
    return visibility, jnp.concatenate(beams, axis=0)


def solution(mesh):
    in_specs = (P("inp", "tm"), P(), P())
    out_specs = (P("tm", "inp", None), P("inp", "tm"))
    return jax.shard_map(
        on_device, mesh=mesh, in_specs=in_specs, out_specs=out_specs, check_vma=False
    )
```

```python
import functools
import math

import jax
import jax.numpy as jnp
from jax import lax
from jax.experimental import pallas as pl
from jax.experimental.pallas import tpu as pltpu
from jax.sharding import PartitionSpec as P

P_SIZE = 512
TAPS = 4
NCH = 128
LANES = 128
ROWS = 8
PIECES = P_SIZE // LANES
VMEM_BYTES = 62 * 1024 * 1024
SMALL_BYTES = 20 * 1024 * 1024


def odd_rows(rows):
    tiles = rows // ROWS
    return (tiles + 1 - tiles % 2) * ROWS


def write_table(chan_ref, table):
    chosen = chan_ref[pl.ds(0, 1), :].astype(jnp.float32)
    chosen = jnp.broadcast_to(chosen, (NCH, LANES)).T.astype(jnp.int32)
    factor = 1.0 / math.sqrt(P_SIZE)
    quarter = P_SIZE // 4
    for n in range(PIECES):
        points = lax.broadcasted_iota(jnp.int32, (NCH, LANES), 1) + n * LANES
        phase = (chosen * points) & (P_SIZE - 1)
        turned = phase + quarter // 2
        quadrant = (turned // quarter) & 3
        x = ((turned & (quarter - 1)) - quarter // 2).astype(jnp.float32)
        x = x * (2.0 * math.pi / P_SIZE)
        z = x * x
        sine = x + x * z * (
            -1.6666654611e-1 + z * (8.3321608736e-3 + z * -1.9515295891e-4)
        )
        cosine = 1.0 - 0.5 * z + z * z * (
            4.166664568298827e-2 + z * (-1.388731625493765e-3 + z * 2.443315711809948e-5)
        )
        odd = (quadrant & 1) == 1
        real = jnp.where(odd, sine, cosine)
        imag = jnp.where(odd, cosine, sine)
        real = jnp.where((quadrant == 1) | (quadrant == 2), -real, real)
        imag = jnp.where(quadrant >= 2, imag, -imag)
        at = pl.ds(n * LANES, LANES)
        table[pl.ds(0, NCH), at] = (real * factor).astype(jnp.bfloat16)
        table[pl.ds(NCH, NCH), at] = (imag * factor).astype(jnp.bfloat16)


def channelize_kernel(opening, groups, plan, volts_ref, *refs):
    if opening:
        chan_hbm, taps_hbm, *refs = refs
        *outs, table_ref, tail_ref, taps_ref, chan_ref, held, filt, spec, sems = refs
    else:
        halo_ref, taps_ref, table_ref, *refs = refs
        *outs, held, filt, spec, sems = refs
    blocks, extent = held.shape[0], held.shape[1]
    span = extent - (TAPS - 1)
    inputs = blocks * ROWS
    slots = NCH // groups
    pitch, depth = odd_rows(span), odd_rows(inputs)
    me = lax.axis_index("inp")

    def copy_of(b):
        if opening:
            source = volts_ref.at[b, pl.ds(volts_ref.shape[1] - extent, extent)]
            target = held.at[b]
        else:
            source = volts_ref.at[b, pl.ds(0, span)]
            target = held.at[b, pl.ds(TAPS - 1, span)]
        return pltpu.make_async_copy(source, target, sems.at[b])

    if opening:
        chan_copy = pltpu.make_async_copy(chan_hbm, chan_ref, sems.at[blocks])
        taps_copy = pltpu.make_async_copy(taps_hbm, taps_ref, sems.at[blocks + 1])
        chan_copy.start()
        taps_copy.start()
    for b in range(blocks):
        copy_of(b).start()
    if opening:
        chan_copy.wait()
        write_table(chan_ref, table_ref)
        taps_copy.wait()

    def one_block(b, carry):
        copy_of(b).wait()
        taps = [
            [
                jnp.broadcast_to(taps_ref[pl.ds(k, 1), pl.ds(n * LANES, LANES)], (ROWS, LANES))
                for n in range(PIECES)
            ]
            for k in range(TAPS)
        ]
        if opening:
            for k in range(TAPS - 1):
                for n in range(PIECES):
                    tail_ref[b, k, n] = held[b, span + k, n].astype(jnp.float32)
            before = [
                [held[b, k, n].astype(jnp.float32) for n in range(PIECES)]
                for k in range(TAPS - 1)
            ]
        else:
            before = [[halo_ref[b, k, n] for n in range(PIECES)] for k in range(TAPS - 1)]

        def filter_step(step, window):
            window = [list(w) for w in window]
            for u in range(ROWS):
                s = step * ROWS + u
                now = [held[b, s + TAPS - 1, n].astype(jnp.float32) for n in range(PIECES)]
                window = window + [now]
                for n in range(PIECES):
                    total = taps[0][n] * window[0][n]
                    for k in range(1, TAPS):
                        total = total + taps[k][n] * window[k][n]
                    filt[n, pl.ds(s, ROWS, stride=pitch), :] = total
                window = window[1:]
            return window

        lax.fori_loop(0, span // ROWS, filter_step, before)

        def transform(pair, carry):
            rows = []
            for e in range(2):
                at = pl.ds(pl.multiple_of((pair * 2 + e) * pitch, ROWS), span)
                line = [filt[n, at, :].astype(jnp.bfloat16) for n in range(PIECES)]
                rows.append(jnp.concatenate(line, axis=1))
            out = lax.dot_general(
                table_ref[...],
                jnp.concatenate(rows, axis=0),
                (((1,), (1,)), ((), ())),
                preferred_element_type=jnp.float32,
            )
            for e in range(2):
                i = b * ROWS + pair * 2 + e
                spec[pl.ds(i, 2 * NCH, stride=depth), :] = out[:, e * span : (e + 1) * span]
            return carry

        return lax.fori_loop(0, ROWS // 2, transform, carry)

    lax.fori_loop(0, blocks, one_block, 0)
    for out, pieces in zip(outs, plan):
        count = out.shape[1]
        for place, (j, first) in enumerate(pieces):
            for q in range(2):
                there = j if opening else me ^ j
                start = (q * NCH + there * slots + first) * depth
                rows = spec[pl.ds(pl.multiple_of(start, depth), count * depth), :]
                rows = rows.reshape(count, depth, span)[:, :inputs]
                out[place, :, pl.ds(q * inputs, inputs), :] = rows.astype(jnp.bfloat16)


def channelize(volts, extra, groups, plan, counts):
    opening = len(extra) == 2
    blocks, spectra = volts.shape[:2]
    span = spectra // 2
    inputs = blocks * ROWS
    whole = pl.BlockSpec(memory_space=pltpu.VMEM)
    far = pl.BlockSpec(memory_space=pltpu.HBM)
    out_shape = [
        jax.ShapeDtypeStruct((len(pieces), count, 2 * inputs, span), jnp.bfloat16)
        for pieces, count in zip(plan, counts)
    ]
    scratch = [
        pltpu.VMEM((blocks, span + TAPS - 1, PIECES, ROWS, LANES), jnp.int32),
        pltpu.VMEM((PIECES, ROWS * odd_rows(span), LANES), jnp.float32),
        pltpu.VMEM((2 * NCH * odd_rows(inputs), span), jnp.float32),
        pltpu.SemaphoreType.DMA((blocks + 2,)),
    ]
    if opening:
        out_shape.append(jax.ShapeDtypeStruct((2 * NCH, P_SIZE), jnp.bfloat16))
        out_shape.append(
            jax.ShapeDtypeStruct((blocks, TAPS - 1, PIECES, ROWS, LANES), jnp.float32)
        )
        out_shape.append(jax.ShapeDtypeStruct((TAPS, P_SIZE), jnp.float32))
        scratch = [pltpu.VMEM(extra[0].shape, jnp.int32)] + scratch
    in_specs = [far, far, far] if opening else [far, whole, whole, whole]
    moved = blocks * ROWS * span * P_SIZE * 4 + 2 * NCH * inputs * span * 2
    return pl.pallas_call(
        functools.partial(channelize_kernel, opening, groups, plan),
        out_shape=out_shape,
        in_specs=in_specs,
        out_specs=[whole] * len(out_shape),
        scratch_shapes=scratch,
        compiler_params=pltpu.CompilerParams(vmem_limit_bytes=VMEM_BYTES),
        cost_estimate=pl.CostEstimate(flops=1000, bytes_accessed=12000000, transcendentals=0),
    )(volts, *extra)


def correlate_kernel(groups, others, first, total, places, *refs):
    *parts, beam, stack, both = refs[-others - 3 :]
    channels = beam.shape[0]
    everyone = parts[0].shape[-1]
    inputs = everyone // groups
    span = beam.shape[1] // 2
    rows_each = everyone // others
    me = lax.axis_index("inp")
    here = lax.axis_index("tm")

    def one_channel(c, carry):
        for j in range(groups):
            at = pl.ds(pl.multiple_of((me ^ j) * inputs, inputs), inputs)
            for h in range(2):
                operand, index, start = (places[j], 0, 0) if h == 0 else (0, me ^ j, first)
                for q in range(2):
                    piece = refs[operand][index, start + c, pl.ds(q * inputs, inputs), :]
                    stack[at, pl.ds((2 * h + q) * span, span)] = piece.astype(stack.dtype)
        values = stack[...].astype(jnp.bfloat16)
        wide = values.astype(jnp.float32)
        power = jnp.sum(wide * wide, axis=0, keepdims=True)
        power = jnp.concatenate(
            [
                power[:, 2 * h * span : (2 * h + 1) * span]
                + power[:, (2 * h + 1) * span : (2 * h + 2) * span]
                for h in range(2)
            ],
            axis=1,
        )
        beam[pl.ds(c, 1), :] = power * (1.0 / everyone)
        turned = jnp.concatenate(
            [
                part
                for h in range(2)
                for part in (
                    values[:, (2 * h + 1) * span : (2 * h + 2) * span],
                    -values[:, 2 * h * span : (2 * h + 1) * span],
                )
            ],
            axis=1,
        )
        both[...] = lax.dot_general(
            jnp.concatenate([values, turned], axis=0),
            values,
            (((1,), (1,)), ((), ())),
            preferred_element_type=jnp.float32,
        )
        col = lax.broadcasted_iota(jnp.int32, (rows_each, everyone), 1)
        row = lax.broadcasted_iota(jnp.int32, (rows_each, everyone), 0)
        for k in range(others):
            base = pl.multiple_of((here ^ k) * rows_each, rows_each)
            real = both[pl.ds(base, rows_each), :]
            imag = both[pl.ds(everyone + base, rows_each), :]
            packed = jnp.where(row + base <= col, real, imag)
            parts[k][c] = (packed * (1.0 / total)).astype(parts[k].dtype)
        return carry

    lax.fori_loop(0, channels, one_channel, 0)


def exchange_order(others):
    order = [0]
    distance = others // 2
    while distance >= 1:
        order = order + [k + distance for k in order]
        distance //= 2
    return order


def correlate(operands, places, groups, first, channels, others, total):
    double, span = operands[0].shape[-2:]
    everyone = double // 2 * groups
    rows_each = everyone // others
    whole = pl.BlockSpec(memory_space=pltpu.VMEM)
    shape = (channels, rows_each, everyone)
    parts = [jax.ShapeDtypeStruct(shape, jnp.float32)]
    parts += [jax.ShapeDtypeStruct(shape, jnp.bfloat16)] * (others - 1)
    held = jnp.bfloat16 if double % 32 == 0 else jnp.float32
    return pl.pallas_call(
        functools.partial(correlate_kernel, groups, others, first, total, places),
        out_shape=parts + [jax.ShapeDtypeStruct((channels, 2 * span), jnp.float32)],
        in_specs=[whole] * len(operands),
        out_specs=[whole] * (others + 1),
        scratch_shapes=[
            pltpu.VMEM((everyone, 4 * span), held),
            pltpu.VMEM((2 * everyone, everyone), jnp.float32),
        ],
        compiler_params=pltpu.CompilerParams(vmem_limit_bytes=SMALL_BYTES),
        cost_estimate=pl.CostEstimate(flops=1000, bytes_accessed=100000000, transcendentals=0),
    )(*operands)


def finish_kernel(cuts, *refs):
    out = refs[-1]
    for at, (first, count) in enumerate(cuts):
        step = (len(refs) - 1) // len(cuts) - 1
        came = refs[len(cuts) + at * step : len(cuts) + (at + 1) * step]
        for c in range(count):
            total = refs[at][c]
            for part in came:
                total = total + part[c].astype(jnp.float32)
            out[:, first + c, :] = total


def finish(kept, came, cuts):
    rows_each, everyone = kept[0].shape[1:]
    slots = sum(count for _, count in cuts)
    whole = pl.BlockSpec(memory_space=pltpu.VMEM)
    return pl.pallas_call(
        functools.partial(finish_kernel, cuts),
        out_shape=jax.ShapeDtypeStruct((rows_each, slots, everyone), jnp.float32),
        in_specs=[whole] * (len(kept) + len(came)),
        out_specs=whole,
        cost_estimate=pl.CostEstimate(flops=1000, bytes_accessed=1000, transcendentals=0),
        compiler_params=pltpu.CompilerParams(vmem_limit_bytes=SMALL_BYTES),
    )(*kept, *came)


def swapped(block, axis, distance):
    devices = range(lax.axis_size(axis))
    return lax.ppermute(block, axis, [(i, i ^ distance) for i in devices])


def after(block, *earlier):
    if not earlier:
        return block
    return lax.optimization_barrier((block, *earlier))[0]


def send_order(groups):
    half = groups // 2
    return list(range(half, groups)) + list(range(1, half))


def channel_cuts(slots):
    sizes = [8, 8] if slots == 16 else [slots]
    firsts = [sum(sizes[:n]) for n in range(len(sizes))]
    return list(zip(firsts, sizes))


def on_device(voltage, taps, chan_table):
    inputs = voltage.shape[0]
    spectra = voltage.shape[1] // P_SIZE
    groups = lax.axis_size("inp")
    others = lax.axis_size("tm")
    slots = NCH // groups
    total = spectra * others
    cuts = channel_cuts(slots)
    volts = voltage.reshape(inputs // ROWS, ROWS, spectra, PIECES, LANES)
    volts = jnp.transpose(volts, (0, 2, 3, 1, 4))

    plan = [[(d, 0) for d in range(groups)]]
    late, table, tail, taps = channelize(
        volts, (chan_table.reshape(-1, LANES), taps), groups, plan, [slots]
    )
    late = lax.all_to_all(late, "inp", split_axis=0, concat_axis=0, tiled=True)
    devices = range(others)
    halo = lax.ppermute(tail, "tm", [(i - 1, i) for i in devices if i > 0])

    plan, counts = [], []
    for first, count in cuts:
        plan += [[(j, first)] for j in range(groups)]
        counts += [count] * groups
    early = channelize(volts, (halo, taps, table), groups, plan, counts)

    order = send_order(groups)
    kept, came, beams = [], [], []
    for at, (first, count) in enumerate(cuts):
        mine = early[at * groups : (at + 1) * groups]
        got = [swapped(mine[j], "inp", j) for j in order]
        operands = [late, mine[0]] + got
        places = [1] + [2 + order.index(j) for j in range(1, groups)]
        *parts, beam = correlate(operands, places, groups, first, count, others, total)
        kept.append(parts[0])
        came.append([swapped(parts[k], "tm", k) for k in reversed(range(1, others))])
        beams.append(beam)
    visibility = finish(kept, sum(came, []), cuts)
    return visibility, jnp.concatenate(beams, axis=0)


def solution(mesh):
    in_specs = (P("inp", "tm"), P(), P())
    out_specs = (P("tm", "inp", None), P("inp", "tm"))
    return jax.shard_map(
        on_device, mesh=mesh, in_specs=in_specs, out_specs=out_specs, check_vma=False
    )
```
